32 devices in a mesh: row: 2 (over core), col: 16 (over z, y, x).
Axes of the slice: x: 2, y: 2, z: 4, core: 2. Of those that a mesh axis runs over, the one named last changes fastest.
Arguments:
- tile_amps: bfloat16 [6144, 6144], P('row', 'col'), as said below
- cycle_ints: bfloat16 [6144, 6144], P('row', 'col'), as said below
- base_ints: bfloat16 [6144, 6144], P('row', 'col'), as said below
- amp_mask: int32 [96, 96], P('row', 'col'), may hold values from 0 to 1, as said below
- int_mask: int32 [96, 96], P('row', 'col'), may hold values from 0 to 1, as said below
- pair_amps: bfloat16 [64, 196608], P(None, ('row', 'col')), may hold values from -6 to 6
- ladder_ints: bfloat16 [196608, 1024], P(('row', 'col')), may hold values from -0.02734375 to 0.02734375
- pair_list: int32 [16], replicated, may hold values from 0 to 63, as said below
Outputs:
- cycle_residual: float32 [6144, 6144], P('row', 'col')
- ladder: float32 [16, 1024], P(None, 'col')
The draws below stay inside these ranges and needn't reach their ends.
Inputs may be any that keep to these rules, and one draw needn't show every extreme that they name: `tile_amps`: equal to its transpose. `cycle_ints`: equal to its transpose. `base_ints`: equal to its transpose. `amp_mask`: 0 or 1, equal to its transpose, 1 on every diagonal tile. `int_mask`: 0 or 1, equal to its transpose, 1 on every diagonal tile. `pair_list`: distinct entries.
All inputs are finite; a program needn't handle non-finite values.
Results may differ from the reference program's by a relative error of at most 0.0029.
Values may be sent and summed in bfloat16 or wider, within the bound.
A program may use at most 128 MiB of HBM per device.

```python
import jax
import jax.numpy as jnp

TILE = 64
AB = 1024
NPAIRS = 64
PAIRS = 16
N = 6144
NT = 96
CD = 196608


def symmetric_mask(key):
    values = jax.random.randint(key, (NT, NT), 0, 100)
    tile_rows = jnp.arange(NT)[:, None]
    tile_cols = jnp.arange(NT)[None, :]
    mirrored = jnp.where(tile_rows <= tile_cols, values, values.T)
    distance = jnp.abs(tile_rows - tile_cols)
    band_width = max(NT // 4, 1)
    threshold = jnp.maximum(10, 85 - 75 * distance // band_width)
    return jnp.where(distance == 0, 1, (mirrored < threshold).astype(jnp.int32)).astype(jnp.int32)


def draw_amp_mask(key, part):
    return symmetric_mask(jax.random.fold_in(key, 11))


def draw_int_mask(key, part):
    return symmetric_mask(jax.random.fold_in(key, 12))


def normal_field(key):
    entries = jax.random.normal(key, (N, N), jnp.float32)
    return (entries + entries.T) * 0.7071


def draw_tile_amps(key, part):
    inner = jax.random.fold_in(key, 21)
    field = normal_field(inner)
    return (field * N ** (-0.5)).astype(jnp.bfloat16)


def draw_cycle_ints(key, part):
    inner = jax.random.fold_in(key, 22)
    field = normal_field(inner)
    return field.astype(jnp.bfloat16)


def draw_base_ints(key, part):
    inner = jax.random.fold_in(key, 23)
    field = normal_field(inner)
    return field.astype(jnp.bfloat16)


def draw_pair_list(key, part):
    first, second = jax.random.split(jax.random.fold_in(key, 31))
    others = jax.random.permutation(first, NPAIRS - 1)[:PAIRS - 1]
    listed = jnp.concatenate([others, jnp.array([NPAIRS - 1])])
    return jax.random.permutation(second, listed).astype(jnp.int32)


def raised(values, own_key, source, target, parts, factor):
    def block_of(axis_at):
        return (jnp.arange(values.shape[axis_at]) // (values.shape[axis_at] // parts)).reshape((-1,) + (1,) * (values.ndim - 1 - axis_at))

    near = jax.random.permutation(own_key, parts)[block_of(target)]
    second = (block_of(target) + parts // 2) % parts
    return jnp.where((block_of(source) == near) | (block_of(source) == second), factor * values, values)


def block_levels(rng, extent, pieces, low, high):
    gain, own = 1.0, jax.random.fold_in(rng, 6)
    for dim, shards_of in pieces:
        draws = jnp.exp(jax.random.uniform(jax.random.fold_in(own, dim), (shards_of,), jnp.float32, low / len(pieces), high / len(pieces)))
        gain = gain * jnp.repeat(draws, extent[dim] // shards_of).reshape([-1 if axis == dim else 1 for axis in range(len(extent))])
    return gain


def scatter_about(rng, shape, scale, most, cuts=(), held_as=jnp.bfloat16):
    drawn = jax.random.normal(rng, shape, jnp.float32) * scale
    if len(cuts) > 0:
        drawn = block_levels(rng, shape, cuts, -0.22, 0.18) * drawn
    return jnp.clip(drawn, min=-most, max=most).astype(held_as)


def noise_with(key, extent, deviation, limit, cuts, heavy, kind=jnp.bfloat16):
    values = deviation * jax.random.normal(key, extent, jnp.float32)
    if cuts:
        values = values * block_levels(key, extent, cuts, -0.22, 0.18)
    return jnp.clip(raised(values, jax.random.fold_in(key, 3), *heavy), -limit, limit).astype(kind)


def setup_inputs(seed: int = 0) -> dict:
    keys = jax.random.split(jax.random.key(seed), 9)
    return {
        "tile_amps": draw_tile_amps(jax.random.fold_in(keys[8], 71), 0),
        "cycle_ints": draw_cycle_ints(jax.random.fold_in(keys[8], 71), 0),
        "base_ints": draw_base_ints(jax.random.fold_in(keys[8], 71), 0),
        "amp_mask": draw_amp_mask(jax.random.fold_in(keys[8], 71), 0),
        "int_mask": draw_int_mask(jax.random.fold_in(keys[8], 71), 0),
        "pair_amps": scatter_about(keys[5], (NPAIRS, CD), 1.0, 6.0, ((1, 32),)),
        "ladder_ints": noise_with(keys[6], (CD, AB), CD ** -0.5, 0.02734375, ((0, 32),), (0, 1, 32, 2.75)),
        "pair_list": draw_pair_list(jax.random.fold_in(keys[8], 71), 0),
    }


def expand(mask, dtype):
    return jnp.repeat(jnp.repeat(mask, TILE, axis=0), TILE, axis=1).astype(dtype)


def reference(tile_amps, cycle_ints, base_ints, amp_mask, int_mask, pair_amps, ladder_ints, pair_list):
    amplitudes = tile_amps * expand(amp_mask, tile_amps.dtype)
    integrals = cycle_ints * expand(int_mask, cycle_ints.dtype)
    baseline = base_ints * expand(int_mask, base_ints.dtype)
    product = jnp.dot(integrals, amplitudes, preferred_element_type=jnp.float32)
    intermediate = (baseline.astype(jnp.float32) + product).astype(tile_amps.dtype)
    cycle_residual = jnp.dot(amplitudes, intermediate, preferred_element_type=jnp.float32)
    chosen = jnp.take(pair_amps, pair_list.astype(jnp.int32), axis=0)
    ladder = jnp.dot(chosen, ladder_ints, preferred_element_type=jnp.float32)
    return cycle_residual, ladder
```

```python
import functools

import jax
import jax.numpy as jnp
from jax import lax
from jax.experimental import pallas as pl
from jax.experimental.pallas import tpu as pltpu
from jax.sharding import PartitionSpec as P

SMEM = pltpu.SMEM
VMEM = pltpu.VMEM
MIB = 1024 * 1024


def widen(mask, field):
    rows, cols = mask.shape
    tile = field.shape[0] // rows
    spread = jnp.broadcast_to(mask.astype(field.dtype)[:, None, :, None], (rows, tile, cols, tile))
    return field * spread.reshape(rows * tile, cols * tile)


def pack_kernel(tile, cap, sel_ref, mask_ref, field_ref, other_ref, out_ref, ids_ref, masked_ref):
    rows, cols = sel_ref.shape
    high = lax.broadcasted_iota(jnp.int32, (tile, 2 * tile), 1) >= tile

    def row(p, count):
        span = pl.ds(pl.multiple_of(p * tile, tile), tile)
        masked_ref[span, :] = other_ref[span, :]
        for c in range(cols):
            lanes = slice(c * tile, (c + 1) * tile)

            @pl.when(mask_ref[p, c] == 0)
            def _():
                masked_ref[span, lanes] = jnp.zeros((tile, tile), masked_ref.dtype)

            chosen = sel_ref[p, c]

            @pl.when((chosen != 0) & (count < cap))
            def _():
                one = field_ref[span, lanes]
                both = jnp.concatenate([one, one], axis=1)
                slot = count // 2
                keep = high | (count % 2 == 0)
                out_ref[slot] = jnp.where(keep, both, out_ref[slot])
                ids_ref[count] = p * 256 + c
                ids_ref[count + 1] = p * 256 + c

            count = count + chosen
        return count

    ids_ref[ids_ref.shape[0] - 1] = lax.fori_loop(0, rows, row, jnp.int32(0))


def pack(tile, cap, length, sel, mask, field, other):
    return pl.pallas_call(
        functools.partial(pack_kernel, tile, cap),
        out_shape=(
            jax.ShapeDtypeStruct((cap // 2, tile, 2 * tile), field.dtype),
            jax.ShapeDtypeStruct((length,), jnp.int32),
            jax.ShapeDtypeStruct(other.shape, other.dtype),
        ),
        in_specs=[
            pl.BlockSpec(memory_space=SMEM),
            pl.BlockSpec(memory_space=SMEM),
            pl.BlockSpec(memory_space=VMEM),
            pl.BlockSpec(memory_space=VMEM),
        ],
        out_specs=(
            pl.BlockSpec(memory_space=VMEM),
            pl.BlockSpec(memory_space=SMEM),
            pl.BlockSpec(memory_space=VMEM),
        ),
        compiler_params=pltpu.CompilerParams(vmem_limit_bytes=24 * MIB),
        name="pack_tiles",
    )(sel, mask, field, other)


def multiply_kernel(tile, cols, span, place_ref, ids_ref, packed_ref, x_ref, *rest):
    if len(rest) == 5:
        base_ref, out_ref, panel, slots, sems = rest
    else:
        base_ref = None
        out_ref, panel, slots, sems = rest
    senders, pairs = packed_ref.shape[:2]
    height, width = panel.shape
    rows = height // tile
    tiles = width // tile
    last = ids_ref.shape[1] - 1
    place = place_ref[0]
    high = lax.broadcasted_iota(jnp.int32, (tile, 2 * tile), 1) // tile

    def fetch(sender):
        return pltpu.make_async_copy(
            packed_ref.at[sender], slots.at[sender % 2], sems.at[sender % 2]
        )

    fetch(0).start()

    @pl.loop(0, rows)
    def _(p):
        panel[pl.ds(pl.multiple_of(p * tile, tile), tile), :] = jnp.zeros(
            (tile, width), panel.dtype
        )

    def put(a, b, both):
        where_rows = pl.ds(pl.multiple_of(a * tile, tile), tile)
        where_cols = pl.ds(pl.multiple_of((b // 2) * (2 * tile), 2 * tile), 2 * tile)
        keep = high == b % 2
        panel[where_rows, where_cols] = jnp.where(keep, both, panel[where_rows, where_cols])

    @pl.loop(0, senders)
    def _(sender):
        fetch(sender).wait()

        @pl.when(sender + 1 < senders)
        def _():
            fetch(sender + 1).start()

        first = sender * cols - place * rows
        first = jnp.where(first < 0, first + tiles, first)
        count = jnp.minimum(ids_ref[sender, last], 2 * pairs)
        used = (count + 1) // 2
        buffer = slots.at[sender % 2]

        def straight(i):
            ida = ids_ref[sender, 2 * i]
            idb = ids_ref[sender, 2 * i + 1]
            pair = buffer[i]
            left = pair[:, :tile]
            right = pair[:, tile:]
            pa, qa = ida // 256, first + ida % 256
            pb, qb = idb // 256, first + idb % 256
            put(pa, qa, jnp.concatenate([left, left], axis=1))
            put(pb, qb, jnp.concatenate([right, right], axis=1))
            return pair, pa, qa, pb, qb

        @pl.when(first < rows)
        def _():
            @pl.loop(0, used)
            def _(i):
                pair, pa, qa, pb, qb = straight(i)
                turned = jnp.concatenate([pair, pair], axis=0).T
                put(qa, pa, turned[:tile])
                put(qb, pb, turned[tile:])

        @pl.when(first >= rows)
        def _():
            @pl.loop(0, used)
            def _(i):
                straight(i)

    @pl.loop(0, height // span)
    def _(m):
        band = pl.ds(pl.multiple_of(m * span, span), span)
        total = jnp.dot(panel[band, :], x_ref[...], preferred_element_type=jnp.float32)
        if base_ref is not None:
            total = total + base_ref[band, :].astype(jnp.float32)
        out_ref[band, :] = total.astype(out_ref.dtype)


def multiply(tile, cols, rows, place, ids, packed, x, base, dtype):
    height, width = rows * tile, x.shape[0]
    span = next(s for s in (512, 256, 128, tile) if height % s == 0)
    operands = [place, ids, packed, x] + ([] if base is None else [base])
    smem, vmem = pl.BlockSpec(memory_space=SMEM), pl.BlockSpec(memory_space=VMEM)
    in_specs = [smem, smem, pl.BlockSpec(memory_space=pl.ANY), vmem] + ([] if base is None else [vmem])
    return pl.pallas_call(
        functools.partial(multiply_kernel, tile, cols, span),
        out_shape=jax.ShapeDtypeStruct((height, x.shape[1]), dtype),
        in_specs=in_specs,
        out_specs=vmem,
        scratch_shapes=[
            pltpu.VMEM((height, width), x.dtype),
            pltpu.VMEM((2,) + packed.shape[1:], packed.dtype),
            pltpu.SemaphoreType.DMA((2,)),
        ],
        compiler_params=pltpu.CompilerParams(vmem_limit_bytes=60 * MIB),
        cost_estimate=pl.CostEstimate(
            flops=2 * height * width * x.shape[1], bytes_accessed=packed.size * 2, transcendentals=0
        ),
        name="multiply_tiles",
    )(*operands)


def own_first(block):
    n = lax.axis_size("row")
    parts = [block]
    for shift in range(1, n):
        parts.append(lax.ppermute(block, "row", [((i + shift) % n, i) for i in range(n)]))
    return jnp.concatenate(parts, axis=0)


def on_device(
    tile_amps, cycle_ints, base_ints, amp_mask, int_mask, pair_amps, ladder_ints, pair_list
):
    rows, cols = amp_mask.shape
    tile = tile_amps.shape[0] // rows
    senders = lax.axis_size("col")
    place = lax.axis_index("row")
    cap = rows * cols // 3 if rows * cols >= 256 else rows * cols
    cap += cap % 2
    length = -(-(cap + 1) // 128) * 128

    p = place * rows + jnp.arange(rows, dtype=jnp.int32)[:, None]
    q = lax.axis_index("col") * cols + jnp.arange(cols, dtype=jnp.int32)[None, :]
    odd = (p + q) % 2 == 1
    sent = jnp.where(q // rows == place, jnp.where(p > q, odd, ~odd), True).astype(jnp.int32)

    ints, int_ids, baseline = pack(tile, cap, length, int_mask * sent, int_mask, cycle_ints, base_ints)
    amps, amp_ids, amplitudes = pack(tile, cap, length, amp_mask * sent, amp_mask, tile_amps, tile_amps)
    both_ids = jnp.stack([int_ids, amp_ids])
    all_ids = lax.all_gather(both_ids, ("row", "col"), axis=0, tiled=False)
    fits = jnp.max(all_ids[:, :, length - 1]) <= cap
    row_ids = lax.dynamic_slice_in_dim(all_ids, place * senders, senders, 0)

    stored = pair_amps.shape[0]
    selector = (pair_list[:, None] == jnp.arange(stored, dtype=jnp.int32)[None, :]).astype(
        jnp.bfloat16
    )
    chosen = jnp.dot(selector, pair_amps, preferred_element_type=jnp.float32).astype(jnp.bfloat16)
    partial_sums = jnp.dot(chosen, ladder_ints, preferred_element_type=jnp.float32)

    def packed_way(partial_sums):
        where = place.reshape(1).astype(jnp.int32)
        int_tiles = lax.all_gather(ints, "col", axis=0, tiled=False)
        amp_tiles = lax.all_gather(amps, "col", axis=0, tiled=False)
        totals = lax.psum(partial_sums, ("row", "col"))
        inter = multiply(
            tile, cols, rows, where, row_ids[:, 0], int_tiles, own_first(amplitudes), baseline,
            jnp.bfloat16,
        )
        residual = multiply(
            tile, cols, rows, where, row_ids[:, 1], amp_tiles, own_first(inter), None, jnp.float32
        )
        return residual, totals

    def whole_way(partial_sums):
        integrals = widen(int_mask, cycle_ints)
        amp_panel = lax.all_gather(amplitudes, "col", axis=1, tiled=True)
        int_columns = lax.all_gather(integrals, "row", axis=0, tiled=True)
        product = jnp.dot(amp_panel, int_columns, preferred_element_type=jnp.float32)
        turned = (baseline.astype(jnp.float32) + product).astype(jnp.bfloat16)
        turned_columns = lax.all_gather(turned, "row", axis=0, tiled=True)
        inter_rows = lax.all_to_all(turned_columns, "col", split_axis=0, concat_axis=1, tiled=True)
        residual = lax.dot_general(
            amp_panel, inter_rows, (((1,), (1,)), ((), ())), preferred_element_type=jnp.float32
        )
        return residual, lax.psum(partial_sums, ("row", "col"))

    if rows % cols == 0:
        cycle_residual, totals = lax.cond(fits, packed_way, whole_way, partial_sums)
    else:
        cycle_residual, totals = whole_way(partial_sums)
    share_width = totals.shape[1] // senders
    ladder = lax.dynamic_slice_in_dim(totals, lax.axis_index("col") * share_width, share_width, 1)
    return (cycle_residual, ladder)


def solution(mesh):
    in_specs = (
        P("row", "col"),
        P("row", "col"),
        P("row", "col"),
        P("row", "col"),
        P("row", "col"),
        P(None, ("row", "col")),
        P(("row", "col"), None),
        P(),
    )
    out_specs = (P("row", "col"), P(None, "col"))
    return jax.shard_map(
        on_device, mesh=mesh, in_specs=in_specs, out_specs=out_specs, check_vma=False
    )
```
